1024 devices in a mesh: ep: 32 (over z, core), tp: 4 (over x), dp: 8 (over y).
Axes of the slice: x: 4, y: 8, z: 16, core: 2. Of those that a mesh axis runs over, the one named last changes fastest.
Arguments:
- latent: bfloat16 [32768, 1024], P(('ep', 'dp')), may hold values from -6 to 6
- cotangent: bfloat16 [32768, 1024], P(('ep', 'dp')), may hold values from -6 to 6
- expert_ids: int32 [32768, 6], P(('ep', 'dp')), may hold values from 0 to 31, all different within a row; in each aligned block of 128 rows (0 to 127, 128 to 255, ...) at most 25 rows name the same one
- route_probs: float32 [32768, 6], P(('ep', 'dp')), may hold values from 0.1 to 0.4
- w_gate: bfloat16 [32, 1024, 1024], P('ep', None, 'tp'), may hold values from -0.1875 to 0.1875
- w_up: bfloat16 [32, 1024, 1024], P('ep', None, 'tp'), may hold values from -0.1875 to 0.1875
- w_down: bfloat16 [32, 1024, 1024], P('ep', 'tp'), may hold values from -0.1875 to 0.1875
Outputs:
- combined: bfloat16 [32768, 1024], P(('ep', 'dp'), 'tp')
- grad_latent: bfloat16 [32768, 1024], P(('ep', 'dp'), 'tp')
- grad_gate: float32 [32, 1024, 1024], P('ep', 'dp', 'tp')
- grad_up: float32 [32, 1024, 1024], P('ep', 'dp', 'tp')
- grad_down: float32 [32, 1024, 1024], P('ep', 'tp', 'dp')
The draws below stay inside these ranges and needn't reach their ends.
Inputs may be any that keep to these rules, and one draw needn't show every extreme that they name: `expert_ids`: each row names 6 different experts. Among the 128 rows of one device no expert is named by more than 25 rows, and in some devices one expert is named by exactly 25.
All inputs are finite; a program needn't handle non-finite values.
Results may differ from the reference program's by a relative error of at most 0.015.
Values may be sent and summed in bfloat16 or wider, within the bound.
A program may use at most 64 MiB of HBM per device.

```python
import math
import jax
import jax.numpy as jnp
import numpy as np
from jax import lax

L = 1024
F = 1024
TOPK = 6
TOK_DEV = 128
EXPERTS = 32
TOKENS = 32768
CAP = 25
N_EP = 32
N_TP = 4
N_DP = 8


def shard_levels(stream_key, shape, pieces, smallest, high):
    factor_of, own = 1.0, jax.random.fold_in(stream_key, 6)
    for dim, parts in pieces:
        steps = jnp.exp(jax.random.uniform(jax.random.fold_in(own, dim), (parts,), jnp.float32, smallest / len(pieces), high / len(pieces)))
        factor_of = factor_of * jnp.repeat(steps, shape[dim] // parts).reshape([-1 if axis == dim else 1 for axis in range(len(shape))])
    return factor_of


def routed_block(key, own, number, rows, number_of, top, bound, lean):
    ranking = jax.random.permutation(key, number_of)
    packed, ordinary = load_shares(number_of, rows * top, bound, lean, True), load_shares(number_of, rows * top, bound, lean, False)
    places = jnp.arange(number_of)

    def named(sizes, offset_by):
        used = int((sizes > 0).sum())
        fixed = max(1, used // 4)
        shifted = fixed + (places - fixed + offset_by * (used - fixed)) % max(1, number_of - fixed)
        return jnp.zeros((number_of,), jnp.int32).at[ranking[jnp.where(places < fixed, places, shifted)]].set(jnp.asarray(sizes, jnp.int32))

    sizes = jnp.where(number % 4 == 0, named(packed, number // 4), named(ordinary, number - number // 4 - 1))
    mixed = jax.random.permutation(jax.random.fold_in(own, 3), number_of)
    donor, receiver = mixed[0:number_of // 2 * 2:2], mixed[1:number_of // 2 * 2:2]
    room = jnp.minimum(sizes[donor] - 1, bound - sizes[receiver]) // 2
    room = jnp.where((donor == ranking[0]) | (receiver == ranking[0]) | (sizes[receiver] == 0), 0, jnp.maximum(room, 0))
    shifted = jax.random.randint(jax.random.fold_in(own, 4), (number_of // 2,), 0, 1 << 20) % (room + 1)
    sizes = sizes.at[donor].add(-shifted).at[receiver].add(shifted)
    members = jnp.searchsorted(jnp.cumsum(sizes), jnp.arange(rows * top), side="right").astype(jnp.int32)
    table = members.reshape(top, rows).T
    table = table[jax.random.permutation(jax.random.fold_in(own, 1), rows)]
    offset_by = jax.random.randint(jax.random.fold_in(own, 2), (rows, 1), 0, top)
    return jnp.take_along_axis(table, (jnp.arange(top)[None, :] + offset_by) % top, axis=1)


def load_shares(number_of, total, limit, slope, full):
    loads = [(1 << 20) // math.isqrt(rank ** slope) + 1 for rank in range(1, number_of + 1)]
    largest = limit if full else min(limit, max(-(-total // number_of), total * loads[0] // sum(loads)))
    least = 1 if total - largest >= number_of - 1 else 0
    given, spare = [largest] + [least] * (number_of - 1), total - largest - least * (number_of - 1)
    while spare > 0:
        free = [i for i in range(1, number_of) if given[i] < largest] or [i for i in range(1, number_of) if given[i] < limit]
        pool, budget = sum([loads[i] for i in free]), spare
        for i in free:
            addition = min(limit - given[i], max(1, budget * loads[i] // pool), spare)
            given[i] = given[i] + addition
            spare = spare - addition
    return np.array(given)


def bell_draw(own_key, shape, spread, most, cuts=(), held_as=jnp.bfloat16):
    drawn = spread * jax.random.normal(own_key, shape, jnp.float32)
    if cuts:
        drawn = drawn * shard_levels(own_key, shape, cuts, -0.22, 0.18)
    return jnp.clip(drawn, -most, most).astype(held_as)


def setup_inputs(seed: int = 0) -> dict:
    seeds = jax.random.split(jax.random.key(seed), 8)
    latent = bell_draw(seeds[0], (TOKENS, L), 1.0, 6.0, ((0, 256),))
    cotangent = bell_draw(seeds[1], (TOKENS, L), 1.0, 6.0, ((0, 256),))
    expert_ids_keys = jax.random.split(jax.random.fold_in(seeds[2], 1), TOKENS // TOK_DEV)
    expert_ids_turns = jax.random.permutation(jax.random.fold_in(seeds[2], 3), TOKENS // TOK_DEV)
    expert_ids = jax.vmap(lambda own, number: routed_block(jax.random.fold_in(seeds[2], 2), own, number, TOK_DEV, EXPERTS, TOPK, CAP, 2))(expert_ids_keys, expert_ids_turns).reshape((TOKENS, TOPK))
    route_probs = jnp.clip(0.1 + 0.3 * jax.random.uniform(seeds[3], (TOKENS, TOPK), jnp.float32) ** shard_levels(seeds[3], (TOKENS, TOPK), ((0, 256),), -0.2, 0.2), 0.1, 0.4)
    w_gate = bell_draw(seeds[4], (EXPERTS, L, F), L ** -0.5, 0.1875, ((0, 32), (2, 4)))
    w_up = bell_draw(seeds[5], (EXPERTS, L, F), L ** -0.5, 0.1875, ((0, 32), (2, 4)))
    w_down = bell_draw(seeds[6], (EXPERTS, F, L), F ** -0.5, 0.1875, ((0, 32), (1, 4)))
    return dict(latent=latent, cotangent=cotangent, expert_ids=expert_ids, route_probs=route_probs, w_gate=w_gate, w_up=w_up, w_down=w_down)


def reference(latent, cotangent, expert_ids, route_probs, w_gate, w_up, w_down):
    tokens = latent.shape[0]
    routes = tokens * TOPK
    blocks = tokens // TOK_DEV
    slot_count = blocks * CAP
    flat_ids = expert_ids.reshape(routes).astype(jnp.int32)
    one_hot = (flat_ids[:, None] == jnp.arange(EXPERTS, dtype=jnp.int32)[None, :]).astype(jnp.int32)
    per_block = one_hot.reshape(blocks, TOK_DEV * TOPK, EXPERTS)
    rank_prior = (jnp.cumsum(per_block, axis=1).astype(jnp.int32) - per_block).astype(jnp.int32)
    position = jnp.sum(rank_prior * per_block, axis=2).astype(jnp.int32).reshape(routes)
    block_of = (jnp.arange(routes, dtype=jnp.int32) // (TOK_DEV * TOPK)).astype(jnp.int32)
    flat_slot = (flat_ids * slot_count + block_of * CAP + position).astype(jnp.int32)
    slot_owner = jnp.full((EXPERTS * slot_count,), routes, jnp.int32)
    slot_owner = slot_owner.at[flat_slot].set(jnp.arange(routes, dtype=jnp.int32)).reshape(EXPERTS, slot_count)
    zero_row = jnp.zeros((1, L), jnp.bfloat16)
    route_rows = jnp.concatenate([jnp.repeat(latent, TOPK, axis=0), zero_row], axis=0)
    scaled = (route_probs.reshape(routes, 1) * jnp.repeat(cotangent, TOPK, axis=0).astype(jnp.float32)).astype(jnp.bfloat16)
    scaled_rows = jnp.concatenate([scaled, zero_row], axis=0)
    group = F // N_TP

    def expert_pass(operands):
        owner_row, gate_weight, up_weight, down_weight = operands
        slot_rows = route_rows[owner_row]
        slot_grads = scaled_rows[owner_row]
        gate_pre = jnp.dot(slot_rows, gate_weight, preferred_element_type=jnp.float32)
        up_value = jnp.dot(slot_rows, up_weight, preferred_element_type=jnp.float32)
        sigmoid_gate = jax.nn.sigmoid(gate_pre)
        activated = gate_pre * sigmoid_gate
        hidden = (activated * up_value).astype(jnp.bfloat16)
        hidden_split = hidden.reshape(slot_count, N_TP, group).astype(jnp.float32)
        down_split = down_weight.reshape(N_TP, group, L).astype(jnp.float32)
        out_split = jnp.einsum("snf,nfl->snl", hidden_split, down_split)
        out_split = lax.optimization_barrier(out_split.astype(jnp.bfloat16)).astype(jnp.float32)
        out_rows = jnp.sum(out_split, axis=1)
        d_hidden = jnp.dot(slot_grads, down_weight.T, preferred_element_type=jnp.float32)
        slope_term = sigmoid_gate * (1.0 + gate_pre * (1.0 - sigmoid_gate))
        d_gate = (d_hidden * up_value * slope_term).astype(jnp.bfloat16)
        d_up = (d_hidden * activated).astype(jnp.bfloat16)
        gate_split = gate_weight.reshape(L, N_TP, group).astype(jnp.float32)
        up_split = up_weight.reshape(L, N_TP, group).astype(jnp.float32)
        back_split = jnp.einsum("snf,lnf->snl", d_gate.reshape(slot_count, N_TP, group).astype(jnp.float32), gate_split)
        back_split = back_split + jnp.einsum("snf,lnf->snl", d_up.reshape(slot_count, N_TP, group).astype(jnp.float32), up_split)
        back_split = lax.optimization_barrier(back_split.astype(jnp.bfloat16)).astype(jnp.float32)
        back_rows = jnp.sum(back_split, axis=1)
        rows_grouped = slot_rows.reshape(N_EP, N_DP, CAP, L).astype(jnp.float32)
        grads_grouped = slot_grads.reshape(N_EP, N_DP, CAP, L).astype(jnp.float32)
        hidden_grouped = hidden.reshape(N_EP, N_DP, CAP, F).astype(jnp.float32)
        gate_terms = jnp.einsum("ikcl,ikcf->klf", rows_grouped, d_gate.reshape(N_EP, N_DP, CAP, F).astype(jnp.float32))
        up_terms = jnp.einsum("ikcl,ikcf->klf", rows_grouped, d_up.reshape(N_EP, N_DP, CAP, F).astype(jnp.float32))
        down_terms = jnp.einsum("ikcf,ikcl->kfl", hidden_grouped, grads_grouped)
        grad_gate_e = jnp.sum(lax.optimization_barrier(gate_terms.astype(jnp.bfloat16)).astype(jnp.float32), axis=0)
        grad_up_e = jnp.sum(lax.optimization_barrier(up_terms.astype(jnp.bfloat16)).astype(jnp.float32), axis=0)
        grad_down_e = jnp.sum(lax.optimization_barrier(down_terms.astype(jnp.bfloat16)).astype(jnp.float32), axis=0)
        return out_rows, back_rows, grad_gate_e, grad_up_e, grad_down_e

    out_slots, back_slots, grad_gate, grad_up, grad_down = lax.map(expert_pass, (slot_owner, w_gate, w_up, w_down))
    out_route = out_slots.reshape(EXPERTS * slot_count, L)[flat_slot].reshape(tokens, TOPK, L)
    back_route = back_slots.reshape(EXPERTS * slot_count, L)[flat_slot].reshape(tokens, TOPK, L)
    combined = jnp.sum(route_probs[:, :, None] * out_route, axis=1).astype(jnp.bfloat16)
    grad_latent = jnp.sum(back_route, axis=1).astype(jnp.bfloat16)
    return combined, grad_latent, grad_gate, grad_up, grad_down
```

```python
import jax
import jax.numpy as jnp
from jax import lax
from jax.experimental import pallas as pl
from jax.experimental.pallas import tpu as pltpu
from jax.sharding import PartitionSpec as P

MESH = pl.DeviceIdType.MESH
BF, F32 = jnp.bfloat16, jnp.float32

NZ, NX, NY = 16, 4, 8
TOK = 128
META = 16
CAP = 25
SLOT = 32
ROWS = 208
HALF = 112
Q = 256
GROUPS = ((2, -2, 3, -3), (4, -4, 5, -5), (6, -6, 7, -7), (1, -1, 8, 0))
INDEX = {(o, f): 8 * g + 2 * i + f for g, group in enumerate(GROUPS) for i, o in enumerate(group) for f in (0, 1)}


def dot(a, b):
    return jnp.dot(a, b, preferred_element_type=F32)


def dot_bt(a, b):
    return lax.dot_general(a, b, (((1,), (1,)), ((), ())), preferred_element_type=F32)


def dot_at(a, b):
    return lax.dot_general(a, b, (((0,), (0,)), ((), ())), preferred_element_type=F32)


def iota(shape, dim):
    return lax.broadcasted_iota(jnp.int32, shape, dim)


def one(condition):
    return jnp.where(condition, 1.0, 0.0)


def body(lat_ref, cot_ref, meta_ref, ids_ref, wg_ref, wu_ref, wd_ref,
         comb_ref, glat_ref, gg_ref, gu_ref, gd_ref,
         blocks, rows_in, parts, via, from_left, from_right, back_out, back_in, y_out, y_in,
         hid_s, dgu_s, prob_s, mask_s, pick_s, place_s, tokens_s, spread_s,
         ring_s, ring_r, gat_s, gat_r, sum_s, sum_r, ret_s, ret_r, y_s, y_r):
    ep, x, y = lax.axis_index("ep"), lax.axis_index("tp"), lax.axis_index("dp")
    z, core = ep // 2, lax.rem(ep, 2)

    def at_z(offset, flip):
        c = 1 - core if flip else core
        return (2 * lax.rem(z + offset + NZ, NZ) + c, x, y)

    def x_at(offset):
        return lax.rem(x + offset + NX, NX)

    def copy(src, dst, send, recv, device):
        return pltpu.make_async_remote_copy(
            src_ref=src, dst_ref=dst, send_sem=send, recv_sem=recv, device_id=device, device_id_type=MESH)

    right, left = (ep, x_at(1), y), (ep, x_at(-1), y)
    sent = []

    def go(c):
        c.start()
        sent.append(c)
        return c

    greeted = [at_z(1, 0), at_z(-1, 0), at_z(0, 1), right, left]
    greeted += [(ep, x, lax.rem(y + i, NY)) for i in range(1, NY)]
    barrier = pltpu.get_barrier_semaphore()
    for device in greeted:
        pl.semaphore_signal(barrier, inc=1, device_id=device, device_id_type=MESH)

    own = INDEX[0, 0]
    columns = pl.ds(pl.multiple_of(x * Q, Q), Q)
    blocks[own, 0:TOK, 0:Q] = lat_ref[:, columns]
    blocks[own, 0:TOK, Q:2 * Q] = cot_ref[:, columns]
    meta = meta_ref[...]
    hi = meta.astype(BF)
    rest = meta - hi.astype(F32)
    mid = rest.astype(BF)
    low = (rest - mid.astype(F32)).astype(BF)
    blocks[own, TOK:TOK + META, 0:128] = hi
    blocks[own, TOK:TOK + META, 128:256] = mid
    blocks[own, TOK:TOK + META, 256:384] = low
    blocks[own, TOK:TOK + META, 384:512] = jnp.zeros((META, 128), BF)
    pl.semaphore_wait(barrier, len(greeted))

    def ring_copy(offset, step):
        src, dst = INDEX[offset, 0], INDEX[offset + step, 0]
        return copy(blocks.at[src], blocks.at[dst], ring_s.at[dst], ring_r.at[dst], at_z(-step, 0))

    def twin_copy(offset):
        src, dst = INDEX[offset, 0], INDEX[offset, 1]
        return copy(blocks.at[src], blocks.at[dst], ring_s.at[dst], ring_r.at[dst], at_z(0, 1))

    arriving, twins = {}, {}
    arriving[1] = go(ring_copy(0, 1))
    arriving[-1] = go(ring_copy(0, -1))
    twins[0] = go(twin_copy(0))

    def ring(distance):
        for sign in (1, -1):
            offset = sign * distance
            if offset == -8:
                continue
            arriving[offset].wait_recv()
            if -7 < offset < 8:
                arriving[offset + sign] = go(ring_copy(offset, sign))
            twins[offset] = go(twin_copy(offset))

    ids = ids_ref[...]
    named = jnp.zeros((TOK, 32), F32)
    for k in range(6):
        named = named + one(ids[:, k:k + 1] == iota((TOK, 32), 1))
    below = one(iota((TOK, TOK), 0) > iota((TOK, TOK), 1)).astype(BF)
    rank = dot(below, named.astype(BF))
    rank = jnp.where(named > 0, rank, -1.0).astype(BF)
    first = 32 * iota((32, 32 * SLOT), 0)
    at = iota((32, 32 * SLOT), 1)
    wide = dot(rank, one((at >= first) & (at < first + SLOT)).astype(BF))
    tokens_s[...] = one(wide == (iota((TOK, 32 * SLOT), 1) & (SLOT - 1)).astype(F32)).astype(BF)
    for j in range(8):
        r, s = iota((SLOT, ROWS), 0), iota((SLOT, ROWS), 1)
        spread_s[j * SLOT:(j + 1) * SLOT, :] = one((s == r + CAP * j) & (r < CAP)).astype(BF)
    above = one(iota((TOK, TOK), 0) < iota((TOK, TOK), 1)).astype(BF)
    mine = ep.astype(F32)

    gathers, sums = {}, {}

    def span(g, part=None):
        if part is None:
            return pl.ds(g * ROWS, ROWS)
        return pl.ds(g * ROWS, HALF) if part == 0 else pl.ds(g * ROWS + HALF, ROWS - HALF)

    def gather_copy(g, i, q, part, device):
        ref = rows_in.at[q, span(g, part)]
        return copy(ref, ref, gat_s.at[6 * g + i], gat_r.at[6 * g + i], device)

    def select(g):
        for offset in GROUPS[g]:
            twins[offset].wait_recv()
        for j in range(8):
            held = blocks[8 * g + j, TOK:TOK + META, 0:384].astype(F32)
            held = held[:, 0:128] + held[:, 128:256] + held[:, 256:384]
            hit = held[0:8] == mine
            mask_s[j:j + 1, :] = jnp.sum(one(hit), axis=0, keepdims=True)
            pick_s[j:j + 1, :] = jnp.sum(jnp.where(hit, held[8:16], 0.0), axis=0, keepdims=True)
        mask = mask_s[...]
        place = dot(mask.astype(BF), above) + (CAP * iota((8, TOK), 0)).astype(F32)
        place_s[...] = jnp.where(mask > 0, place, -1.0)
        row = iota((ROWS, TOK), 0).astype(F32)
        prob = jnp.zeros((ROWS, TOK), F32)
        total = jnp.zeros((ROWS, 2 * Q), F32)
        for j in range(8):
            chosen = row == place_s[j:j + 1, :]
            prob = prob + jnp.where(chosen, pick_s[j:j + 1, :], 0.0)
            total = total + dot(one(chosen).astype(BF), blocks[8 * g + j, 0:TOK, :])
        prob = jnp.sum(prob, axis=1, keepdims=True)
        prob_s[span(g), :] = prob
        rows_in[x, span(g), 0:Q] = total[:, 0:Q].astype(BF)
        rows_in[x, span(g), Q:2 * Q] = (total[:, Q:2 * Q] * prob).astype(BF)
        gathers[g, 0] = go(gather_copy(g, 0, x, 0, right))
        gathers[g, 1] = go(gather_copy(g, 1, x, 1, left))
        gathers[g, 2] = go(gather_copy(g, 2, x, 1, right))
        gathers[g, 3] = go(gather_copy(g, 3, x, 0, left))

    def forward(g):
        gathers[g, 0].wait_recv()
        gathers[g, 4] = go(gather_copy(g, 4, x_at(-1), 0, right))
        gathers[g, 1].wait_recv()
        gathers[g, 5] = go(gather_copy(g, 5, x_at(1), 1, left))

    def sum_copy(g, i, src, dst, device):
        return copy(src, dst, sum_s.at[6 * g + i], sum_r.at[6 * g + i], device)

    def part_at(g, q, part):
        return parts.at[q, span(g, part)]

    def compute(g):
        for i in (2, 3, 4, 5):
            gathers[g, i].wait_recv()
        gate = jnp.zeros((ROWS, Q), F32)
        up = jnp.zeros((ROWS, Q), F32)
        d_hidden = jnp.zeros((ROWS, Q), F32)
        for q in range(NX):
            latent = rows_in[q, span(g), 0:Q]
            gate = gate + dot(latent, wg_ref[q * Q:(q + 1) * Q, :])
            up = up + dot(latent, wu_ref[q * Q:(q + 1) * Q, :])
            d_hidden = d_hidden + dot_bt(rows_in[q, span(g), Q:2 * Q], wd_ref[:, q * Q:(q + 1) * Q])
        sigmoid = jax.nn.sigmoid(gate)
        activated = gate * sigmoid
        hidden = (activated * up).astype(BF)
        slope = sigmoid * (1.0 + gate * (1.0 - sigmoid))
        d_gate = (d_hidden * up * slope).astype(BF)
        d_up = (d_hidden * activated).astype(BF)
        hid_s[span(g), :] = hidden
        dgu_s[span(g), 0:Q] = d_gate
        dgu_s[span(g), Q:2 * Q] = d_up
        for q in range(NX):
            parts[q, span(g), 0:Q] = dot(hidden, wd_ref[:, q * Q:(q + 1) * Q]).astype(BF)
            back = dot_bt(d_gate, wg_ref[q * Q:(q + 1) * Q, :]) + dot_bt(d_up, wu_ref[q * Q:(q + 1) * Q, :])
            parts[q, span(g), Q:2 * Q] = back.astype(BF)
        sums[g, 0] = go(sum_copy(g, 0, part_at(g, x_at(2), 0), via.at[span(g, 0)], right))
        sums[g, 1] = go(sum_copy(g, 1, part_at(g, x_at(2), 1), via.at[span(g, 1)], left))
        sums[g, 2] = go(sum_copy(g, 2, part_at(g, x_at(1), 1), from_left.at[span(g, 1)], right))
        sums[g, 3] = go(sum_copy(g, 3, part_at(g, x_at(-1), 0), from_right.at[span(g, 0)], left))

    def pass_on(g):
        for part, q, dst, device in ((0, x_at(1), from_left, right), (1, x_at(-1), from_right, left)):
            sums[g, part].wait_recv()
            here = span(g, part)
            parts[q, here, :] = (parts[q, here, :].astype(F32) + via[here, :].astype(F32)).astype(BF)
            sums[g, 4 + part] = go(sum_copy(g, 4 + part, part_at(g, q, part), dst.at[here], device))

    returns = []

    def give_back(g):
        for i in (2, 3, 4, 5):
            sums[g, i].wait_recv()
        here = span(g)
        total = parts[x, here, :].astype(F32) + from_left[here, :].astype(F32) + from_right[here, :].astype(F32)
        scaled = (total[:, 0:Q] * prob_s[here, :]).astype(BF)
        spread = spread_s[...]
        base = 8 * g * SLOT
        back_out[base:base + 8 * SLOT, 0:Q] = dot(spread, scaled).astype(BF)
        back_out[base:base + 8 * SLOT, Q:2 * Q] = dot(spread, total[:, Q:2 * Q].astype(BF)).astype(BF)
        target = pl.ds(pl.multiple_of(ep * SLOT, SLOT), SLOT)
        for offset in GROUPS[g]:
            for flip in (0, 1):
                i = INDEX[offset, flip]
                if i == own:
                    back_in[target, :] = back_out[i * SLOT:(i + 1) * SLOT, :]
                    continue
                returns.append(go(copy(back_out.at[pl.ds(i * SLOT, SLOT)], back_in.at[target],
                                       ret_s.at[i], ret_r.at[i], at_z(offset, flip))))

    trades = []

    def weight_gradients():
        for q in range(NX):
            both = dot_at(rows_in[q, :, 0:Q], dgu_s[...]).astype(BF)
            down = dot_at(hid_s[...], rows_in[q, :, Q:2 * Q]).astype(BF)
            for h in (0, 1):
                for c in range(4):
                    y_out[2 * q + h, c * 128:(c + 1) * 128, :] = both[h * 128:(h + 1) * 128, c * 128:(c + 1) * 128]
                y_out[2 * q + h, 512:768, :] = down[:, h * 128:(h + 1) * 128]
        for i in range(1, NY):
            to = lax.rem(y + i, NY)
            trades.append(go(copy(y_out.at[to], y_in.at[y], y_s.at[i], y_r.at[i], (ep, x, to))))

    ring(1)
    ring(2)
    ring(3)
    select(0)
    ring(4)
    forward(0)
    ring(5)
    select(1)
    ring(6)
    compute(0)
    forward(1)
    ring(7)
    ring(8)
    select(2)
    pass_on(0)
    compute(1)
    forward(2)
    select(3)
    give_back(0)
    pass_on(1)
    compute(2)
    forward(3)
    give_back(1)
    pass_on(2)
    compute(3)
    weight_gradients()
    give_back(2)
    pass_on(3)
    give_back(3)

    y_in[y] = y_out[y]
    for trade in trades:
        trade.wait_recv()
    sum_y = jnp.zeros((768, 128), F32)
    for i in range(NY):
        sum_y = sum_y + y_in[i].astype(F32)
    gg_ref[:, 0:128] = sum_y[0:128]
    gg_ref[:, 128:256] = sum_y[128:256]
    gu_ref[:, 0:128] = sum_y[256:384]
    gu_ref[:, 128:256] = sum_y[384:512]
    gd_ref[...] = sum_y[512:768]
    for c in returns:
        c.wait_recv()
    result = dot(tokens_s[...], back_in[...])
    comb_ref[...] = result[:, 0:Q].astype(BF)
    glat_ref[...] = result[:, Q:2 * Q].astype(BF)
    for c in sent:
        c.wait_send()


def local(latent, cotangent, expert_ids, route_probs, w_gate, w_up, w_down):
    meta = jnp.concatenate([
        expert_ids.T.astype(F32), jnp.full((2, TOK), -1.0, F32), route_probs.T, jnp.zeros((2, TOK), F32)], axis=0)
    vmem = pl.BlockSpec(memory_space=pltpu.VMEM)
    dma = pltpu.SemaphoreType.DMA
    comb, glat, gg, gu, gd = pl.pallas_call(
        body,
        out_shape=(
            jax.ShapeDtypeStruct((TOK, Q), BF), jax.ShapeDtypeStruct((TOK, Q), BF),
            jax.ShapeDtypeStruct((128, Q), F32), jax.ShapeDtypeStruct((128, Q), F32),
            jax.ShapeDtypeStruct((Q, 128), F32)),
        in_specs=[vmem] * 7,
        out_specs=(vmem,) * 5,
        scratch_shapes=[
            pltpu.VMEM((32, TOK + META, 2 * Q), BF),
            pltpu.VMEM((NX, 4 * ROWS, 2 * Q), BF),
            pltpu.VMEM((NX, 4 * ROWS, 2 * Q), BF),
            pltpu.VMEM((4 * ROWS, 2 * Q), BF),
            pltpu.VMEM((4 * ROWS, 2 * Q), BF),
            pltpu.VMEM((4 * ROWS, 2 * Q), BF),
            pltpu.VMEM((32 * SLOT, 2 * Q), BF),
            pltpu.VMEM((32 * SLOT, 2 * Q), BF),
            pltpu.VMEM((NY, 768, 128), BF),
            pltpu.VMEM((NY, 768, 128), BF),
            pltpu.VMEM((4 * ROWS, Q), BF),
            pltpu.VMEM((4 * ROWS, 2 * Q), BF),
            pltpu.VMEM((4 * ROWS, 1), F32),
            pltpu.VMEM((8, TOK), F32),
            pltpu.VMEM((8, TOK), F32),
            pltpu.VMEM((8, TOK), F32),
            pltpu.VMEM((TOK, 32 * SLOT), BF),
            pltpu.VMEM((8 * SLOT, ROWS), BF),
            dma((32,)), dma((32,)), dma((24,)), dma((24,)), dma((24,)), dma((24,)),
            dma((32,)), dma((32,)), dma((NY,)), dma((NY,)),
        ],
        compiler_params=pltpu.CompilerParams(collective_id=0, has_side_effects=True, vmem_limit_bytes=56 * 2**20),
        cost_estimate=pl.CostEstimate(flops=4 * 10**9, bytes_accessed=8 * 2**20, transcendentals=10**6),
        name="moe",
    )(latent, cotangent, meta, expert_ids, w_gate[0], w_up[0], w_down[0])
    return comb, glat, gg[None], gu[None], gd[None]


def solution(mesh):
    return jax.shard_map(
        local,
        mesh=mesh,
        in_specs=(
            P(("ep", "dp"), None), P(("ep", "dp"), None), P(("ep", "dp"), None), P(("ep", "dp"), None),
            P("ep", None, "tp"), P("ep", None, "tp"), P("ep", "tp", None),
        ),
        out_specs=(
            P(("ep", "dp"), "tp"), P(("ep", "dp"), "tp"), P("ep", "dp", "tp"), P("ep", "dp", "tp"), P("ep", "tp", "dp"),
        ),
        check_vma=False,
    )
```

```python
import jax
import jax.numpy as jnp
from jax import lax
from jax.experimental import pallas as pl
from jax.experimental.pallas import tpu as pltpu
from jax.sharding import PartitionSpec as P

MESH = pl.DeviceIdType.MESH
BF, F32 = jnp.bfloat16, jnp.float32

NZ, NX, NY = 16, 4, 8
TOK = 128
META = 16
CAP = 25
SLOT = 112
Q = 256
CHUNKS = (0, 64, TOK + META)
GROUPS = ((2, -2), (3, -3, 4, -4), (5, -5, 6, -6), (7, -7, 8), (1, -1, 0))
FIRST = [2 * sum(len(group) for group in GROUPS[:g]) for g in range(len(GROUPS) + 1)]
INDEX = {(o, f): FIRST[g] + 2 * i + f for g, group in enumerate(GROUPS) for i, o in enumerate(group) for f in (0, 1)}
BLOCKS = [2 * len(group) for group in GROUPS]
MOST = max(BLOCKS)
ROWS = [-(-CAP * n // 16) * 16 for n in BLOCKS]
HALF = [-(-rows // 32) * 16 for rows in ROWS]
START = [sum(ROWS[:g]) for g in range(len(GROUPS) + 1)]
ALL = START[-1]
ORDER = "r1.0 r1.1 r2.0 s4 r2.1 r3.0 s0 r3.1 r4.0 f4 f0 r4.1 r5.0 s1 r5.1 c0 r6.0 f1 r6.1 r7.0 p0 s2 g0 f2 c1 r7.1 p1 c2 r8.0 r8.1 g1 p2 s3 g2 f3 c4 c3 w0 p4 p3 g4 g3"
FIRST_COMPUTED = int(ORDER[ORDER.index("c") + 1])


def dot(a, b):
    return jnp.dot(a, b, preferred_element_type=F32)


def dot_bt(a, b):
    return lax.dot_general(a, b, (((1,), (1,)), ((), ())), preferred_element_type=F32)


def dot_at(a, b):
    return lax.dot_general(a, b, (((0,), (0,)), ((), ())), preferred_element_type=F32)


def iota(shape, dim):
    return lax.broadcasted_iota(jnp.int32, shape, dim)


def one(condition):
    return jnp.where(condition, 1.0, 0.0)


def body(lat_ref, cot_ref, ids_ref, probs_ref, wg_hbm, wu_hbm, wd_hbm,
         comb_ref, glat_ref, gg_ref, gu_ref, gd_ref,
         blocks, rows_in, parts, via, from_left, from_right, back_out, back_in, y_out, y_in,
         hid_s, dgu_s, prob_s, mask_s, pick_s, place_s, tokens_s, spread_s,
         wg_ref, wu_ref, wd_ref, load_s, ring_s, ring_r, gat_s, gat_r, sum_s, sum_r, ret_s, ret_r, y_s, y_r):
    ep, x, y = lax.axis_index("ep"), lax.axis_index("tp"), lax.axis_index("dp")
    z, core = ep // 2, lax.rem(ep, 2)

    def at_z(offset, flip):
        c = 1 - core if flip else core
        return (2 * lax.rem(z + offset + NZ, NZ) + c, x, y)

    def x_at(offset):
        return lax.rem(x + offset + NX, NX)

    def copy(src, dst, send, recv, device):
        return pltpu.make_async_remote_copy(
            src_ref=src, dst_ref=dst, send_sem=send, recv_sem=recv, device_id=device, device_id_type=MESH)

    right, left = (ep, x_at(1), y), (ep, x_at(-1), y)
    sent = []

    def go(c):
        c.start()
        sent.append(c)
        return c

    own = INDEX[0, 0]
    columns = pl.ds(pl.multiple_of(x * Q, Q), Q)
    loads = [
        pltpu.make_async_copy(lat_ref.at[:, columns], blocks.at[own, pl.ds(0, TOK), pl.ds(0, Q)], load_s.at[0]),
        pltpu.make_async_copy(cot_ref.at[:, columns], blocks.at[own, pl.ds(0, TOK), pl.ds(Q, Q)], load_s.at[1]),
        pltpu.make_async_copy(wg_hbm, wg_ref, load_s.at[2]),
        pltpu.make_async_copy(wu_hbm, wu_ref, load_s.at[3]),
        pltpu.make_async_copy(wd_hbm, wd_ref, load_s.at[4]),
    ]
    for c in loads:
        c.start()

    greeted = [at_z(1, 0), at_z(-1, 0), at_z(0, 1), right, left]
    greeted += [(ep, x, lax.rem(y + i, NY)) for i in range(1, NY)]
    barrier = pltpu.get_barrier_semaphore()
    for device in greeted:
        pl.semaphore_signal(barrier, inc=1, device_id=device, device_id_type=MESH)

    meta = jnp.concatenate([
        ids_ref[...].astype(F32), jnp.full((2, TOK), -1.0, F32), probs_ref[...], jnp.zeros((2, TOK), F32)], axis=0)
    hi = meta.astype(BF)
    rest = meta - hi.astype(F32)
    mid = rest.astype(BF)
    low = (rest - mid.astype(F32)).astype(BF)
    blocks[own, TOK:TOK + META, 0:128] = hi
    blocks[own, TOK:TOK + META, 128:256] = mid
    blocks[own, TOK:TOK + META, 256:384] = low
    blocks[own, TOK:TOK + META, 384:512] = jnp.zeros((META, 128), BF)
    for c in loads[:2]:
        c.wait()
    pl.semaphore_wait(barrier, len(greeted))

    def ring_copy(offset, step, c):
        src, dst, part = INDEX[offset, 0], INDEX[offset + step, 0], pl.ds(CHUNKS[c], CHUNKS[c + 1] - CHUNKS[c])
        return copy(blocks.at[src, part], blocks.at[dst, part], ring_s.at[dst, c], ring_r.at[dst, c], at_z(-step, 0))

    def twin_copy(offset, c):
        src, dst, part = INDEX[offset, 0], INDEX[offset, 1], pl.ds(CHUNKS[c], CHUNKS[c + 1] - CHUNKS[c])
        return copy(blocks.at[src, part], blocks.at[dst, part], ring_s.at[dst, c], ring_r.at[dst, c], at_z(0, 1))

    arriving, twins = {}, {}
    pieces = range(len(CHUNKS) - 1)
    for c in pieces:
        arriving[1, c] = go(ring_copy(0, 1, c))
        arriving[-1, c] = go(ring_copy(0, -1, c))
    for c in pieces:
        twins[0, c] = go(twin_copy(0, c))

    def ring(distance, only=None):
        for c in pieces if only is None else (only,):
            for sign in (1, -1):
                offset = sign * distance
                if offset == -8:
                    continue
                arriving[offset, c].wait_recv()
                if -7 < offset < 8:
                    arriving[offset + sign, c] = go(ring_copy(offset, sign, c))
                twins[offset, c] = go(twin_copy(offset, c))

    ids = ids_ref[...]
    named = jnp.zeros((32, TOK), F32)
    for k in range(6):
        named = named + one(ids[k:k + 1, :] == iota((32, TOK), 0))
    above = one(iota((TOK, TOK), 0) < iota((TOK, TOK), 1)).astype(BF)
    rank = dot(named.astype(BF), above)
    rank = jnp.where(named > 0, rank, -1024.0).astype(BF)
    first = SLOT * iota((32, 32 * SLOT), 0)
    at = iota((32, 32 * SLOT), 1)
    inside = (at >= first) & (at < first + SLOT)
    wide = dot_at(rank, one(inside).astype(BF))
    within = jnp.sum(jnp.where(inside, at - first, 0), axis=0, keepdims=True).astype(F32)
    for c in range(4):
        tokens_s[c] = one(wide + float(CAP * c) == within).astype(BF)
        for j in range(MOST):
            r, s = iota((SLOT, max(ROWS)), 0) - CAP * c, iota((SLOT, max(ROWS)), 1)
            spread_s[c, j * SLOT:(j + 1) * SLOT, :] = one((s == r + CAP * j) & (r >= 0) & (r < CAP)).astype(BF)
    mine = ep.astype(F32)

    gathers, sums = {}, {}

    def span(g, part=None):
        if part is None:
            return pl.ds(START[g], ROWS[g])
        return pl.ds(START[g], HALF[g]) if part == 0 else pl.ds(START[g] + HALF[g], ROWS[g] - HALF[g])

    def gather_copy(g, i, q, part, device):
        ref = rows_in.at[q, span(g, part)]
        return copy(ref, ref, gat_s.at[6 * g + i], gat_r.at[6 * g + i], device)

    def select(g):
        count, rows = BLOCKS[g], ROWS[g]
        for offset in GROUPS[g]:
            for c in pieces:
                twins[offset, c].wait_recv()
        for j in range(count):
            held = blocks[FIRST[g] + j, TOK:TOK + META, 0:384].astype(F32)
            held = held[:, 0:128] + held[:, 128:256] + held[:, 256:384]
            hit = held[0:8] == mine
            mask_s[j:j + 1, :] = jnp.sum(one(hit), axis=0, keepdims=True)
            pick_s[j:j + 1, :] = jnp.sum(jnp.where(hit, held[8:16], 0.0), axis=0, keepdims=True)
        mask = mask_s[0:count, :]
        place = dot(mask.astype(BF), above) + (CAP * iota((count, TOK), 0)).astype(F32)
        place_s[0:count, :] = jnp.where(mask > 0, place, -1.0)
        row = iota((rows, TOK), 0).astype(F32)
        prob = jnp.zeros((rows, TOK), F32)
        total = jnp.zeros((rows, 2 * Q), F32)
        for j in range(count):
            chosen = row == place_s[j:j + 1, :]
            prob = prob + jnp.where(chosen, pick_s[j:j + 1, :], 0.0)
            total = total + dot(one(chosen).astype(BF), blocks[FIRST[g] + j, 0:TOK, :])
        prob = jnp.sum(prob, axis=1, keepdims=True)
        prob_s[span(g), :] = prob
        rows_in[x, span(g), 0:Q] = total[:, 0:Q].astype(BF)
        rows_in[x, span(g), Q:2 * Q] = (total[:, Q:2 * Q] * prob).astype(BF)
        gathers[g, 0] = go(gather_copy(g, 0, x, 0, right))
        gathers[g, 1] = go(gather_copy(g, 1, x, 1, left))
        gathers[g, 2] = go(gather_copy(g, 2, x, 1, right))
        gathers[g, 3] = go(gather_copy(g, 3, x, 0, left))

    def forward(g):
        gathers[g, 0].wait_recv()
        gathers[g, 4] = go(gather_copy(g, 4, x_at(-1), 0, right))
        gathers[g, 1].wait_recv()
        gathers[g, 5] = go(gather_copy(g, 5, x_at(1), 1, left))

    def sum_copy(g, i, src, dst, device):
        return copy(src, dst, sum_s.at[6 * g + i], sum_r.at[6 * g + i], device)

    def part_at(g, q, part):
        return parts.at[q, span(g, part)]

    def compute(g):
        for i in (2, 3, 4, 5):
            gathers[g, i].wait_recv()
        if g == FIRST_COMPUTED:
            for c in loads[2:]:
                c.wait()
        gate = jnp.zeros((ROWS[g], Q), F32)
        up = jnp.zeros((ROWS[g], Q), F32)
        d_hidden = jnp.zeros((ROWS[g], Q), F32)
        for q in range(NX):
            latent = rows_in[q, span(g), 0:Q]
            gate = gate + dot(latent, wg_ref[q * Q:(q + 1) * Q, :])
            up = up + dot(latent, wu_ref[q * Q:(q + 1) * Q, :])
            d_hidden = d_hidden + dot_bt(rows_in[q, span(g), Q:2 * Q], wd_ref[:, q * Q:(q + 1) * Q])
        sigmoid = jax.nn.sigmoid(gate)
        activated = gate * sigmoid
        hidden = (activated * up).astype(BF)
        slope = sigmoid * (1.0 + gate * (1.0 - sigmoid))
        d_gate = (d_hidden * up * slope).astype(BF)
        d_up = (d_hidden * activated).astype(BF)
        hid_s[span(g), :] = hidden
        dgu_s[span(g), 0:Q] = d_gate
        dgu_s[span(g), Q:2 * Q] = d_up
        for q in range(NX):
            parts[q, span(g), 0:Q] = dot(hidden, wd_ref[:, q * Q:(q + 1) * Q]).astype(BF)
            back = dot_bt(d_gate, wg_ref[q * Q:(q + 1) * Q, :]) + dot_bt(d_up, wu_ref[q * Q:(q + 1) * Q, :])
            parts[q, span(g), Q:2 * Q] = back.astype(BF)
        sums[g, 0] = go(sum_copy(g, 0, part_at(g, x_at(2), 0), via.at[span(g, 0)], right))
        sums[g, 1] = go(sum_copy(g, 1, part_at(g, x_at(2), 1), via.at[span(g, 1)], left))
        sums[g, 2] = go(sum_copy(g, 2, part_at(g, x_at(1), 1), from_left.at[span(g, 1)], right))
        sums[g, 3] = go(sum_copy(g, 3, part_at(g, x_at(-1), 0), from_right.at[span(g, 0)], left))

    def pass_on(g):
        for part, q, dst, device in ((0, x_at(1), from_left, right), (1, x_at(-1), from_right, left)):
            sums[g, part].wait_recv()
            here = span(g, part)
            parts[q, here, :] = (parts[q, here, :].astype(F32) + via[here, :].astype(F32)).astype(BF)
            sums[g, 4 + part] = go(sum_copy(g, 4 + part, part_at(g, q, part), dst.at[here], device))

    returns = []

    def give_back(g):
        for i in (2, 3, 4, 5):
            sums[g, i].wait_recv()
        here = span(g)
        total = parts[x, here, :].astype(F32) + from_left[here, :].astype(F32) + from_right[here, :].astype(F32)
        scaled = (total[:, 0:Q] * prob_s[here, :]).astype(BF)
        plain = total[:, Q:2 * Q].astype(BF)
        size = BLOCKS[g] * SLOT
        packed = jnp.zeros((size, 128), F32)
        for c, values in enumerate((scaled[:, 0:128], scaled[:, 128:256], plain[:, 0:128], plain[:, 128:256])):
            packed = packed + dot(spread_s[c, 0:size, 0:ROWS[g]], values)
        back_out[FIRST[g] * SLOT:FIRST[g] * SLOT + size, :] = packed.astype(BF)
        target = pl.ds(pl.multiple_of(ep * SLOT, SLOT), SLOT)
        for offset in GROUPS[g]:
            for flip in (0, 1):
                i = INDEX[offset, flip]
                if i == own:
                    back_in[target, :] = back_out[i * SLOT:(i + 1) * SLOT, :]
                    continue
                returns.append(go(copy(back_out.at[pl.ds(i * SLOT, SLOT)], back_in.at[target],
                                       ret_s.at[i], ret_r.at[i], at_z(offset, flip))))

    trades = []

    def weight_gradients(_):
        for q in range(NX):
            both = dot_at(rows_in[q, :, 0:Q], dgu_s[...]).astype(BF)
            down = dot_at(hid_s[...], rows_in[q, :, Q:2 * Q]).astype(BF)
            for h in (0, 1):
                for c in range(4):
                    y_out[2 * q + h, c * 128:(c + 1) * 128, :] = both[h * 128:(h + 1) * 128, c * 128:(c + 1) * 128]
                y_out[2 * q + h, 512:768, :] = down[:, h * 128:(h + 1) * 128]
        for i in range(1, NY):
            to = lax.rem(y + i, NY)
            trades.append(go(copy(y_out.at[to], y_in.at[y], y_s.at[i], y_r.at[i], (ep, x, to))))

    steps = dict(r=ring, s=select, f=forward, c=compute, p=pass_on, g=give_back, w=weight_gradients)
    for word in ORDER.split():
        steps[word[0]](*[int(n) for n in word[1:].split(".")])

    y_in[y] = y_out[y]
    for trade in trades:
        trade.wait_recv()
    sum_y = jnp.zeros((768, 128), F32)
    for i in range(NY):
        sum_y = sum_y + y_in[i].astype(F32)
    gg_ref[0, :, 0:128] = sum_y[0:128]
    gg_ref[0, :, 128:256] = sum_y[128:256]
    gu_ref[0, :, 0:128] = sum_y[256:384]
    gu_ref[0, :, 128:256] = sum_y[384:512]
    gd_ref[0] = sum_y[512:768]
    for c in returns:
        c.wait_recv()
    for c, (ref, half) in enumerate(((comb_ref, 0), (comb_ref, 1), (glat_ref, 0), (glat_ref, 1))):
        ref[:, half * 128:(half + 1) * 128] = dot(tokens_s[c], back_in[...]).astype(BF)
    for c in sent:
        c.wait_send()


def local(latent, cotangent, expert_ids, route_probs, w_gate, w_up, w_down):
    vmem, anywhere = pl.BlockSpec(memory_space=pltpu.VMEM), pl.BlockSpec(memory_space=pl.ANY)
    dma = pltpu.SemaphoreType.DMA
    groups = len(GROUPS)
    shapes = (
        jax.ShapeDtypeStruct((TOK, Q), BF), jax.ShapeDtypeStruct((TOK, Q), BF),
        jax.ShapeDtypeStruct((1, 128, Q), F32), jax.ShapeDtypeStruct((1, 128, Q), F32),
        jax.ShapeDtypeStruct((1, Q, 128), F32))
    results = pl.pallas_call(
        body,
        out_shape=shapes,
        in_specs=[anywhere, anywhere, vmem, vmem, anywhere, anywhere, anywhere],
        out_specs=(vmem,) * 5,
        scratch_shapes=[
            pltpu.VMEM((32, TOK + META, 2 * Q), BF),
            pltpu.VMEM((NX, ALL, 2 * Q), BF),
            pltpu.VMEM((NX, ALL, 2 * Q), BF),
            pltpu.VMEM((ALL, 2 * Q), BF),
            pltpu.VMEM((ALL, 2 * Q), BF),
            pltpu.VMEM((ALL, 2 * Q), BF),
            pltpu.VMEM((32 * SLOT, 128), BF),
            pltpu.VMEM((32 * SLOT, 128), BF),
            pltpu.VMEM((NY, 768, 128), BF),
            pltpu.VMEM((NY, 768, 128), BF),
            pltpu.VMEM((ALL, Q), BF),
            pltpu.VMEM((ALL, 2 * Q), BF),
            pltpu.VMEM((ALL, 1), F32),
            pltpu.VMEM((16, TOK), F32),
            pltpu.VMEM((16, TOK), F32),
            pltpu.VMEM((16, TOK), F32),
            pltpu.VMEM((4, TOK, 32 * SLOT), BF),
            pltpu.VMEM((4, MOST * SLOT, max(ROWS)), BF),
            pltpu.VMEM((4 * Q, Q), BF), pltpu.VMEM((4 * Q, Q), BF), pltpu.VMEM((Q, 4 * Q), BF),
            dma((5,)), dma((32, len(CHUNKS) - 1)), dma((32, len(CHUNKS) - 1)),
            dma((6 * groups,)), dma((6 * groups,)), dma((6 * groups,)), dma((6 * groups,)),
            dma((32,)), dma((32,)), dma((NY,)), dma((NY,)),
        ],
        compiler_params=pltpu.CompilerParams(collective_id=0, has_side_effects=True, vmem_limit_bytes=56 * 2**20),
        cost_estimate=pl.CostEstimate(flops=4 * 10**9, bytes_accessed=8 * 2**20, transcendentals=10**6),
        name="moe",
    )(latent, cotangent, expert_ids.T, route_probs.T, w_gate[0], w_up[0], w_down[0])
    return pl.pallas_call(
        hand_over,
        out_shape=shapes,
        in_specs=[vmem] * 5,
        out_specs=(vmem,) * 5,
        name="results",
    )(*results)


def hand_over(*refs):
    for i in range(5):
        refs[5 + i][...] = refs[i][...]


def solution(mesh):
    return jax.shard_map(
        local,
        mesh=mesh,
        in_specs=(
            P(("ep", "dp"), None), P(("ep", "dp"), None), P(("ep", "dp"), None), P(("ep", "dp"), None),
            P("ep", None, "tp"), P("ep", None, "tp"), P("ep", "tp", None),
        ),
        out_specs=(
            P(("ep", "dp"), "tp"), P(("ep", "dp"), "tp"), P("ep", "dp", "tp"), P("ep", "dp", "tp"), P("ep", "tp", "dp"),
        ),
        check_vma=False,
    )
```

```python
import jax
import jax.numpy as jnp
from jax import lax
from jax.experimental import pallas as pl
from jax.experimental.pallas import tpu as pltpu
from jax.sharding import PartitionSpec as P

MESH = pl.DeviceIdType.MESH
BF, F32 = jnp.bfloat16, jnp.float32

NZ, NX, NY = 16, 4, 8
TOK = 128
META = 16
CAP = 25
SLOT = 112
Q = 256
CHUNKS = (0, 64, TOK + META)
GROUPS = ((2, -2, 3, -3), (8, 7, -7), (5, -5, 6, -6), (4, -4), (1, -1, 0))
FIRST = [2 * sum(len(group) for group in GROUPS[:g]) for g in range(len(GROUPS) + 1)]
INDEX = {(o, f): FIRST[g] + 2 * i + f for g, group in enumerate(GROUPS) for i, o in enumerate(group) for f in (0, 1)}
BLOCKS = [2 * len(group) for group in GROUPS]
MOST = max(BLOCKS)
ROWS = [-(-CAP * n // 16) * 16 for n in BLOCKS]
HALF = [-(-rows // 32) * 16 for rows in ROWS]
START = [sum(ROWS[:g]) for g in range(len(GROUPS) + 1)]
ALL = START[-1]
ORDER = "r1.0 r1.1 r2.0 r2.1 s4 r3.0 r3.1 f4 r4.0 s0 r4.1 r5.0 s3 r5.1 r6.0 f0 r6.1 r7.0 f3 s2 r7.1 r8.0 r8.1 f2 s1 c2 p2 f1 c3 c4 g2 c1 p3 c0 w0 g3 p0 p1 g0 p4 g1 g4"
FIRST_COMPUTED = int(ORDER[ORDER.index("c") + 1])


def dot(a, b):
    return jnp.dot(a, b, preferred_element_type=F32)


def dot_bt(a, b):
    return lax.dot_general(a, b, (((1,), (1,)), ((), ())), preferred_element_type=F32)


def dot_at(a, b):
    return lax.dot_general(a, b, (((0,), (0,)), ((), ())), preferred_element_type=F32)


def iota(shape, dim):
    return lax.broadcasted_iota(jnp.int32, shape, dim)


def one(condition):
    return jnp.where(condition, 1.0, 0.0)


def body(lat_ref, cot_ref, ids_ref, probs_ref, wg_hbm, wu_hbm, wd_hbm,
         comb_ref, glat_ref, gg_ref, gu_ref, gd_ref,
         blocks, rows_in, parts, via, from_left, from_right, back_out, back_in, y_out, y_in,
         hid_s, dgu_s, prob_s, mask_s, pick_s, place_s, tokens_s, spread_s,
         wg_ref, wu_ref, wd_ref, load_s, ring_s, ring_r, gat_s, gat_r, sum_s, sum_r, ret_s, ret_r, y_s, y_r):
    ep, x, y = lax.axis_index("ep"), lax.axis_index("tp"), lax.axis_index("dp")
    z, core = ep // 2, lax.rem(ep, 2)

    def at_z(offset, flip):
        c = 1 - core if flip else core
        return (2 * lax.rem(z + offset + NZ, NZ) + c, x, y)

    def x_at(offset):
        return lax.rem(x + offset + NX, NX)

    def copy(src, dst, send, recv, device):
        return pltpu.make_async_remote_copy(
            src_ref=src, dst_ref=dst, send_sem=send, recv_sem=recv, device_id=device, device_id_type=MESH)

    right, left = (ep, x_at(1), y), (ep, x_at(-1), y)
    sent = []

    def go(c):
        c.start()
        sent.append(c)
        return c

    own = INDEX[0, 0]
    columns = pl.ds(pl.multiple_of(x * Q, Q), Q)
    loads = [
        pltpu.make_async_copy(lat_ref.at[:, columns], blocks.at[own, pl.ds(0, TOK), pl.ds(0, Q)], load_s.at[0]),
        pltpu.make_async_copy(cot_ref.at[:, columns], blocks.at[own, pl.ds(0, TOK), pl.ds(Q, Q)], load_s.at[1]),
        pltpu.make_async_copy(wg_hbm, wg_ref, load_s.at[2]),
        pltpu.make_async_copy(wu_hbm, wu_ref, load_s.at[3]),
        pltpu.make_async_copy(wd_hbm, wd_ref, load_s.at[4]),
    ]
    for c in loads:
        c.start()

    greeted = [at_z(1, 0), at_z(-1, 0), at_z(0, 1), right, left]
    greeted += [(ep, x, lax.rem(y + i, NY)) for i in range(1, NY)]
    barrier = pltpu.get_barrier_semaphore()
    for device in greeted:
        pl.semaphore_signal(barrier, inc=1, device_id=device, device_id_type=MESH)

    meta = jnp.concatenate([
        ids_ref[...].astype(F32), jnp.full((2, TOK), -1.0, F32), probs_ref[...], jnp.zeros((2, TOK), F32)], axis=0)
    hi = meta.astype(BF)
    rest = meta - hi.astype(F32)
    mid = rest.astype(BF)
    low = (rest - mid.astype(F32)).astype(BF)
    blocks[own, TOK:TOK + META, 0:128] = hi
    blocks[own, TOK:TOK + META, 128:256] = mid
    blocks[own, TOK:TOK + META, 256:384] = low
    blocks[own, TOK:TOK + META, 384:512] = jnp.zeros((META, 128), BF)
    for c in loads[:2]:
        c.wait()
    pl.semaphore_wait(barrier, len(greeted))

    def ring_copy(offset, step, c):
        src, dst = INDEX[offset, 0], INDEX[8 if offset + step == -8 else offset + step, 0]
        part = pl.ds(CHUNKS[c], CHUNKS[c + 1] - CHUNKS[c])
        return copy(blocks.at[src, part], blocks.at[dst, part], ring_s.at[dst, c], ring_r.at[dst, c], at_z(-step, 0))

    def twin_copy(offset, c):
        src, dst, part = INDEX[offset, 0], INDEX[offset, 1], pl.ds(CHUNKS[c], CHUNKS[c + 1] - CHUNKS[c])
        return copy(blocks.at[src, part], blocks.at[dst, part], ring_s.at[dst, c], ring_r.at[dst, c], at_z(0, 1))

    arriving, twins = {}, {}
    pieces = range(len(CHUNKS) - 1)
    for c in pieces:
        arriving[1, c] = go(ring_copy(0, 1, c))
        arriving[-1, c] = go(ring_copy(0, -1, c))
    for c in pieces:
        twins[0, c] = go(twin_copy(0, c))

    def ring(distance, only=None):
        for c in pieces if only is None else (only,):
            for offset in (distance, -distance) if distance < 8 else (8,):
                arriving[offset, c].wait_recv()
                step = 1 if offset > 0 else -1
                if distance < 7:
                    arriving[offset + step, c] = go(ring_copy(offset, step, c))
                elif distance == 7 and step == 1 - 2 * (c % 2):
                    arriving[8, c] = go(ring_copy(offset, step, c))
                twins[offset, c] = go(twin_copy(offset, c))

    ids = ids_ref[...]
    named = jnp.zeros((32, TOK), F32)
    for k in range(6):
        named = named + one(ids[k:k + 1, :] == iota((32, TOK), 0))
    above = one(iota((TOK, TOK), 0) < iota((TOK, TOK), 1)).astype(BF)
    rank = dot(named.astype(BF), above)
    rank = jnp.where(named > 0, rank, -1024.0).astype(BF)
    first = SLOT * iota((32, 32 * SLOT), 0)
    at = iota((32, 32 * SLOT), 1)
    inside = (at >= first) & (at < first + SLOT)
    wide = dot_at(rank, one(inside).astype(BF))
    within = jnp.sum(jnp.where(inside, at - first, 0), axis=0, keepdims=True).astype(F32)
    for c in range(4):
        tokens_s[c] = one(wide + float(CAP * c) == within).astype(BF)
        for j in range(MOST):
            r, s = iota((SLOT, max(ROWS)), 0) - CAP * c, iota((SLOT, max(ROWS)), 1)
            spread_s[c, j * SLOT:(j + 1) * SLOT, :] = one((s == r + CAP * j) & (r >= 0) & (r < CAP)).astype(BF)
    mine = ep.astype(F32)

    gathers, sums = {}, {}

    def span(g, part=None):
        if part is None:
            return pl.ds(START[g], ROWS[g])
        return pl.ds(START[g], HALF[g]) if part == 0 else pl.ds(START[g] + HALF[g], ROWS[g] - HALF[g])

    def gather_copy(g, i, q, part, device):
        ref = rows_in.at[q, span(g, part)]
        return copy(ref, ref, gat_s.at[6 * g + i], gat_r.at[6 * g + i], device)

    def select(g):
        count, rows = BLOCKS[g], ROWS[g]
        for offset in GROUPS[g]:
            for c in pieces:
                twins[offset, c].wait_recv()
        for j in range(count):
            held = blocks[FIRST[g] + j, TOK:TOK + META, 0:384].astype(F32)
            held = held[:, 0:128] + held[:, 128:256] + held[:, 256:384]
            hit = held[0:8] == mine
            mask_s[j:j + 1, :] = jnp.sum(one(hit), axis=0, keepdims=True)
            pick_s[j:j + 1, :] = jnp.sum(jnp.where(hit, held[8:16], 0.0), axis=0, keepdims=True)
        mask = mask_s[0:count, :]
        place = dot(mask.astype(BF), above) + (CAP * iota((count, TOK), 0)).astype(F32)
        place_s[0:count, :] = jnp.where(mask > 0, place, -1.0)
        row = iota((rows, TOK), 0).astype(F32)
        prob = jnp.zeros((rows, TOK), F32)
        total = jnp.zeros((rows, 2 * Q), F32)
        for j in range(count):
            chosen = row == place_s[j:j + 1, :]
            prob = prob + jnp.where(chosen, pick_s[j:j + 1, :], 0.0)
            total = total + dot(one(chosen).astype(BF), blocks[FIRST[g] + j, 0:TOK, :])
        prob = jnp.sum(prob, axis=1, keepdims=True)
        prob_s[span(g), :] = prob
        rows_in[x, span(g), 0:Q] = total[:, 0:Q].astype(BF)
        rows_in[x, span(g), Q:2 * Q] = (total[:, Q:2 * Q] * prob).astype(BF)
        gathers[g, 0] = go(gather_copy(g, 0, x, 0, right))
        gathers[g, 1] = go(gather_copy(g, 1, x, 1, left))
        gathers[g, 2] = go(gather_copy(g, 2, x, 1, right))
        gathers[g, 3] = go(gather_copy(g, 3, x, 0, left))

    def forward(g):
        gathers[g, 0].wait_recv()
        gathers[g, 4] = go(gather_copy(g, 4, x_at(-1), 0, right))
        gathers[g, 1].wait_recv()
        gathers[g, 5] = go(gather_copy(g, 5, x_at(1), 1, left))

    def sum_copy(g, i, src, dst, device):
        return copy(src, dst, sum_s.at[6 * g + i], sum_r.at[6 * g + i], device)

    def part_at(g, q, part):
        return parts.at[q, span(g, part)]

    def compute(g):
        for i in (2, 3, 4, 5):
            gathers[g, i].wait_recv()
        if g == FIRST_COMPUTED:
            for c in loads[2:]:
                c.wait()
        gate = jnp.zeros((ROWS[g], Q), F32)
        up = jnp.zeros((ROWS[g], Q), F32)
        d_hidden = jnp.zeros((ROWS[g], Q), F32)
        for q in range(NX):
            latent = rows_in[q, span(g), 0:Q]
            gate = gate + dot(latent, wg_ref[q * Q:(q + 1) * Q, :])
            up = up + dot(latent, wu_ref[q * Q:(q + 1) * Q, :])
            d_hidden = d_hidden + dot_bt(rows_in[q, span(g), Q:2 * Q], wd_ref[:, q * Q:(q + 1) * Q])
        sigmoid = jax.nn.sigmoid(gate)
        activated = gate * sigmoid
        hidden = (activated * up).astype(BF)
        slope = sigmoid * (1.0 + gate * (1.0 - sigmoid))
        d_gate = (d_hidden * up * slope).astype(BF)
        d_up = (d_hidden * activated).astype(BF)
        hid_s[span(g), :] = hidden
        dgu_s[span(g), 0:Q] = d_gate
        dgu_s[span(g), Q:2 * Q] = d_up
        for q in range(NX):
            parts[q, span(g), 0:Q] = dot(hidden, wd_ref[:, q * Q:(q + 1) * Q]).astype(BF)
            back = dot_bt(d_gate, wg_ref[q * Q:(q + 1) * Q, :]) + dot_bt(d_up, wu_ref[q * Q:(q + 1) * Q, :])
            parts[q, span(g), Q:2 * Q] = back.astype(BF)
        sums[g, 0] = go(sum_copy(g, 0, part_at(g, x_at(2), 0), via.at[span(g, 0)], right))
        sums[g, 1] = go(sum_copy(g, 1, part_at(g, x_at(2), 1), via.at[span(g, 1)], left))
        sums[g, 2] = go(sum_copy(g, 2, part_at(g, x_at(1), 1), from_left.at[span(g, 1)], right))
        sums[g, 3] = go(sum_copy(g, 3, part_at(g, x_at(-1), 0), from_right.at[span(g, 0)], left))

    def pass_on(g):
        for part, q, dst, device in ((0, x_at(1), from_left, right), (1, x_at(-1), from_right, left)):
            sums[g, part].wait_recv()
            here = span(g, part)
            parts[q, here, :] = (parts[q, here, :].astype(F32) + via[here, :].astype(F32)).astype(BF)
            sums[g, 4 + part] = go(sum_copy(g, 4 + part, part_at(g, q, part), dst.at[here], device))

    returns = []

    def give_back(g):
        for i in (2, 3, 4, 5):
            sums[g, i].wait_recv()
        here = span(g)
        total = parts[x, here, :].astype(F32) + from_left[here, :].astype(F32) + from_right[here, :].astype(F32)
        scaled = (total[:, 0:Q] * prob_s[here, :]).astype(BF)
        plain = total[:, Q:2 * Q].astype(BF)
        size = BLOCKS[g] * SLOT
        packed = jnp.zeros((size, 128), F32)
        for c, values in enumerate((scaled[:, 0:128], scaled[:, 128:256], plain[:, 0:128], plain[:, 128:256])):
            packed = packed + dot(spread_s[c, 0:size, 0:ROWS[g]], values)
        back_out[FIRST[g] * SLOT:FIRST[g] * SLOT + size, :] = packed.astype(BF)
        target = pl.ds(pl.multiple_of(ep * SLOT, SLOT), SLOT)
        for offset in GROUPS[g]:
            for flip in (0, 1):
                i = INDEX[offset, flip]
                if i == own:
                    back_in[target, :] = back_out[i * SLOT:(i + 1) * SLOT, :]
                    continue
                returns.append(go(copy(back_out.at[pl.ds(i * SLOT, SLOT)], back_in.at[target],
                                       ret_s.at[i], ret_r.at[i], at_z(offset, flip))))

    trades = []

    def weight_gradients(_):
        for q in range(NX):
            both = dot_at(rows_in[q, :, 0:Q], dgu_s[...]).astype(BF)
            down = dot_at(hid_s[...], rows_in[q, :, Q:2 * Q]).astype(BF)
            for h in (0, 1):
                for c in range(4):
                    y_out[2 * q + h, c * 128:(c + 1) * 128, :] = both[h * 128:(h + 1) * 128, c * 128:(c + 1) * 128]
                y_out[2 * q + h, 512:768, :] = down[:, h * 128:(h + 1) * 128]
        for i in range(1, NY):
            to = lax.rem(y + i, NY)
            trades.append(go(copy(y_out.at[to], y_in.at[y], y_s.at[i], y_r.at[i], (ep, x, to))))

    steps = dict(r=ring, s=select, f=forward, c=compute, p=pass_on, g=give_back, w=weight_gradients)
    for word in ORDER.split():
        steps[word[0]](*[int(n) for n in word[1:].split(".")])

    y_in[y] = y_out[y]
    for trade in trades:
        trade.wait_recv()
    sum_y = jnp.zeros((768, 128), F32)
    for i in range(NY):
        sum_y = sum_y + y_in[i].astype(F32)
    gg_ref[0, :, 0:128] = sum_y[0:128]
    gg_ref[0, :, 128:256] = sum_y[128:256]
    gu_ref[0, :, 0:128] = sum_y[256:384]
    gu_ref[0, :, 128:256] = sum_y[384:512]
    gd_ref[0] = sum_y[512:768]
    for c in returns:
        c.wait_recv()
    for c, (ref, half) in enumerate(((comb_ref, 0), (comb_ref, 1), (glat_ref, 0), (glat_ref, 1))):
        ref[:, half * 128:(half + 1) * 128] = dot(tokens_s[c], back_in[...]).astype(BF)
    for c in sent:
        c.wait_send()


def local(latent, cotangent, expert_ids, route_probs, w_gate, w_up, w_down):
    vmem, anywhere = pl.BlockSpec(memory_space=pltpu.VMEM), pl.BlockSpec(memory_space=pl.ANY)
    dma = pltpu.SemaphoreType.DMA
    groups = len(GROUPS)
    shapes = (
        jax.ShapeDtypeStruct((TOK, Q), BF), jax.ShapeDtypeStruct((TOK, Q), BF),
        jax.ShapeDtypeStruct((1, 128, Q), F32), jax.ShapeDtypeStruct((1, 128, Q), F32),
        jax.ShapeDtypeStruct((1, Q, 128), F32))
    results = pl.pallas_call(
        body,
        out_shape=shapes,
        in_specs=[anywhere, anywhere, vmem, vmem, anywhere, anywhere, anywhere],
        out_specs=(vmem,) * 5,
        scratch_shapes=[
            pltpu.VMEM((32, TOK + META, 2 * Q), BF),
            pltpu.VMEM((NX, ALL, 2 * Q), BF),
            pltpu.VMEM((NX, ALL, 2 * Q), BF),
            pltpu.VMEM((ALL, 2 * Q), BF),
            pltpu.VMEM((ALL, 2 * Q), BF),
            pltpu.VMEM((ALL, 2 * Q), BF),
            pltpu.VMEM((32 * SLOT, 128), BF),
            pltpu.VMEM((32 * SLOT, 128), BF),
            pltpu.VMEM((NY, 768, 128), BF),
            pltpu.VMEM((NY, 768, 128), BF),
            pltpu.VMEM((ALL, Q), BF),
            pltpu.VMEM((ALL, 2 * Q), BF),
            pltpu.VMEM((ALL, 1), F32),
            pltpu.VMEM((16, TOK), F32),
            pltpu.VMEM((16, TOK), F32),
            pltpu.VMEM((16, TOK), F32),
            pltpu.VMEM((4, TOK, 32 * SLOT), BF),
            pltpu.VMEM((4, MOST * SLOT, max(ROWS)), BF),
            pltpu.VMEM((4 * Q, Q), BF), pltpu.VMEM((4 * Q, Q), BF), pltpu.VMEM((Q, 4 * Q), BF),
            dma((5,)), dma((32, len(CHUNKS) - 1)), dma((32, len(CHUNKS) - 1)),
            dma((6 * groups,)), dma((6 * groups,)), dma((6 * groups,)), dma((6 * groups,)),
            dma((32,)), dma((32,)), dma((NY,)), dma((NY,)),
        ],
        compiler_params=pltpu.CompilerParams(collective_id=0, has_side_effects=True, vmem_limit_bytes=56 * 2**20),
        cost_estimate=pl.CostEstimate(flops=4 * 10**9, bytes_accessed=8 * 2**20, transcendentals=10**6),
        name="moe",
    )(latent, cotangent, expert_ids.T, route_probs.T, w_gate[0], w_up[0], w_down[0])
    return pl.pallas_call(
        hand_over,
        out_shape=shapes,
        in_specs=[vmem] * 5,
        out_specs=(vmem,) * 5,
        name="results",
    )(*results)


def hand_over(*refs):
    for i in range(5):
        refs[5 + i][...] = refs[i][...]


def solution(mesh):
    return jax.shard_map(
        local,
        mesh=mesh,
        in_specs=(
            P(("ep", "dp"), None), P(("ep", "dp"), None), P(("ep", "dp"), None), P(("ep", "dp"), None),
            P("ep", None, "tp"), P("ep", None, "tp"), P("ep", "tp", None),
        ),
        out_specs=(
            P(("ep", "dp"), "tp"), P(("ep", "dp"), "tp"), P("ep", "dp", "tp"), P("ep", "dp", "tp"), P("ep", "tp", "dp"),
        ),
        check_vma=False,
    )
```

```python
import jax
import jax.numpy as jnp
from jax import lax
from jax.experimental import pallas as pl
from jax.experimental.pallas import tpu as pltpu
from jax.sharding import PartitionSpec as P

MESH = pl.DeviceIdType.MESH
BF, F32 = jnp.bfloat16, jnp.float32

NZ, NX, NY = 16, 4, 8
TOK = 128
META = 16
CAP = 25
SLOT = 112
Q = 256
CHUNKS = (0, 64, TOK + META)
GROUPS = ((1, -1, 0), (2, -2, 3, -3), (4, -4, 5, -5), (6, -6), (7, -7, 8))
FIRST = [2 * sum(len(group) for group in GROUPS[:g]) for g in range(len(GROUPS) + 1)]
INDEX = {(o, f): FIRST[g] + 2 * i + f for g, group in enumerate(GROUPS) for i, o in enumerate(group) for f in (0, 1)}
BLOCKS = [2 * len(group) for group in GROUPS]
MOST = max(BLOCKS)
ROWS = [-(-CAP * n // 16) * 16 for n in BLOCKS]
HALF = [-(-rows // 32) * 16 for rows in ROWS]
START = [sum(ROWS[:g]) for g in range(len(GROUPS) + 1)]
ALL = START[-1]
ORDER = "r1.0 r1.1 r2.0 r2.1 s0 r3.0 r3.1 f0 r4.0 s1 r4.1 r5.0 r5.1 f1 s2 r6.0 c1 r6.1 s3 r7.0 r7.1 r8.0 p1 r8.1 f3 s4 c3 f4 g1 f2 p3 c4 c0 g3 p4 c2 w0 p0 g4 g0 p2 g2"
FIRST_COMPUTED = int(ORDER[ORDER.index("c") + 1])


def dot(a, b):
    return jnp.dot(a, b, preferred_element_type=F32)


def dot_bt(a, b):
    return lax.dot_general(a, b, (((1,), (1,)), ((), ())), preferred_element_type=F32)


def dot_at(a, b):
    return lax.dot_general(a, b, (((0,), (0,)), ((), ())), preferred_element_type=F32)


def iota(shape, dim):
    return lax.broadcasted_iota(jnp.int32, shape, dim)


def one(condition):
    return jnp.where(condition, 1.0, 0.0)


def body(lat_ref, cot_ref, ids_ref, probs_ref, wg_hbm, wu_hbm, wd_hbm,
         comb_ref, glat_ref, gg_ref, gu_ref, gd_ref,
         blocks, rows_in, parts, via, from_left, from_right, back_out, back_in, y_out, y_in,
         hid_s, dgu_s, prob_s, mask_s, pick_s, place_s, tokens_s, spread_s,
         wg_ref, wu_ref, wd_ref, load_s, ring_s, ring_r, gat_s, gat_r, sum_s, sum_r, ret_s, ret_r, y_s, y_r):
    ep, x, y = lax.axis_index("ep"), lax.axis_index("tp"), lax.axis_index("dp")
    z, core = ep // 2, lax.rem(ep, 2)

    def at_z(offset, flip):
        c = 1 - core if flip else core
        return (2 * lax.rem(z + offset + NZ, NZ) + c, x, y)

    def x_at(offset):
        return lax.rem(x + offset + NX, NX)

    def copy(src, dst, send, recv, device):
        return pltpu.make_async_remote_copy(
            src_ref=src, dst_ref=dst, send_sem=send, recv_sem=recv, device_id=device, device_id_type=MESH)

    right, left = (ep, x_at(1), y), (ep, x_at(-1), y)
    sent = []

    def go(c):
        c.start()
        sent.append(c)
        return c

    own = INDEX[0, 0]
    columns = pl.ds(pl.multiple_of(x * Q, Q), Q)
    loads = [
        pltpu.make_async_copy(lat_ref.at[:, columns], blocks.at[own, pl.ds(0, TOK), pl.ds(0, Q)], load_s.at[0]),
        pltpu.make_async_copy(cot_ref.at[:, columns], blocks.at[own, pl.ds(0, TOK), pl.ds(Q, Q)], load_s.at[1]),
        pltpu.make_async_copy(wg_hbm, wg_ref, load_s.at[2]),
        pltpu.make_async_copy(wu_hbm, wu_ref, load_s.at[3]),
        pltpu.make_async_copy(wd_hbm, wd_ref, load_s.at[4]),
    ]
    for c in loads:
        c.start()

    greeted = [at_z(1, 0), at_z(-1, 0), at_z(0, 1), right, left]
    greeted += [(ep, x, lax.rem(y + i, NY)) for i in range(1, NY)]
    barrier = pltpu.get_barrier_semaphore()
    for device in greeted:
        pl.semaphore_signal(barrier, inc=1, device_id=device, device_id_type=MESH)

    meta = jnp.concatenate([
        ids_ref[...].astype(F32), jnp.full((2, TOK), -1.0, F32), probs_ref[...], jnp.zeros((2, TOK), F32)], axis=0)
    hi = meta.astype(BF)
    rest = meta - hi.astype(F32)
    mid = rest.astype(BF)
    low = (rest - mid.astype(F32)).astype(BF)
    blocks[own, TOK:TOK + META, 0:128] = hi
    blocks[own, TOK:TOK + META, 128:256] = mid
    blocks[own, TOK:TOK + META, 256:384] = low
    blocks[own, TOK:TOK + META, 384:512] = jnp.zeros((META, 128), BF)
    for c in loads[:2]:
        c.wait()
    pl.semaphore_wait(barrier, len(greeted))

    def ring_copy(offset, step, c):
        src, dst = INDEX[offset, 0], INDEX[8 if offset + step == -8 else offset + step, 0]
        part = pl.ds(CHUNKS[c], CHUNKS[c + 1] - CHUNKS[c])
        return copy(blocks.at[src, part], blocks.at[dst, part], ring_s.at[dst, c], ring_r.at[dst, c], at_z(-step, 0))

    def twin_copy(offset, c):
        src, dst, part = INDEX[offset, 0], INDEX[offset, 1], pl.ds(CHUNKS[c], CHUNKS[c + 1] - CHUNKS[c])
        return copy(blocks.at[src, part], blocks.at[dst, part], ring_s.at[dst, c], ring_r.at[dst, c], at_z(0, 1))

    arriving, twins = {}, {}
    pieces = range(len(CHUNKS) - 1)
    for c in pieces:
        arriving[1, c] = go(ring_copy(0, 1, c))
        arriving[-1, c] = go(ring_copy(0, -1, c))
    for c in pieces:
        twins[0, c] = go(twin_copy(0, c))

    def ring(distance, only=None):
        for c in pieces if only is None else (only,):
            for offset in (distance, -distance) if distance < 8 else (8,):
                arriving[offset, c].wait_recv()
                step = 1 if offset > 0 else -1
                if distance < 7:
                    arriving[offset + step, c] = go(ring_copy(offset, step, c))
                elif distance == 7 and step == 1 - 2 * (c % 2):
                    arriving[8, c] = go(ring_copy(offset, step, c))
                twins[offset, c] = go(twin_copy(offset, c))

    ids = ids_ref[...]
    named = jnp.zeros((32, TOK), F32)
    for k in range(6):
        named = named + one(ids[k:k + 1, :] == iota((32, TOK), 0))
    above = one(iota((TOK, TOK), 0) < iota((TOK, TOK), 1)).astype(BF)
    rank = dot(named.astype(BF), above)
    rank = jnp.where(named > 0, rank, -1024.0).astype(BF)
    first = SLOT * iota((32, 32 * SLOT), 0)
    at = iota((32, 32 * SLOT), 1)
    inside = (at >= first) & (at < first + SLOT)
    wide = dot_at(rank, one(inside).astype(BF))
    within = jnp.sum(jnp.where(inside, at - first, 0), axis=0, keepdims=True).astype(F32)
    for c in range(4):
        tokens_s[c] = one(wide + float(CAP * c) == within).astype(BF)
        for j in range(MOST):
            r, s = iota((SLOT, max(ROWS)), 0) - CAP * c, iota((SLOT, max(ROWS)), 1)
            spread_s[c, j * SLOT:(j + 1) * SLOT, :] = one((s == r + CAP * j) & (r >= 0) & (r < CAP)).astype(BF)
    mine = ep.astype(F32)

    gathers, sums = {}, {}

    def span(g, part=None):
        if part is None:
            return pl.ds(START[g], ROWS[g])
        return pl.ds(START[g], HALF[g]) if part == 0 else pl.ds(START[g] + HALF[g], ROWS[g] - HALF[g])

    def gather_copy(g, i, q, part, device):
        ref = rows_in.at[q, span(g, part)]
        return copy(ref, ref, gat_s.at[6 * g + i], gat_r.at[6 * g + i], device)

    def select(g):
        count, rows = BLOCKS[g], ROWS[g]
        for offset in GROUPS[g]:
            for c in pieces:
                twins[offset, c].wait_recv()
        for j in range(count):
            held = blocks[FIRST[g] + j, TOK:TOK + META, 0:384].astype(F32)
            held = held[:, 0:128] + held[:, 128:256] + held[:, 256:384]
            hit = held[0:8] == mine
            mask_s[j:j + 1, :] = jnp.sum(one(hit), axis=0, keepdims=True)
            pick_s[j:j + 1, :] = jnp.sum(jnp.where(hit, held[8:16], 0.0), axis=0, keepdims=True)
        mask = mask_s[0:count, :]
        place = dot(mask.astype(BF), above) + (CAP * iota((count, TOK), 0)).astype(F32)
        place_s[0:count, :] = jnp.where(mask > 0, place, -1.0)
        row = iota((rows, TOK), 0).astype(F32)
        prob = jnp.zeros((rows, TOK), F32)
        total = jnp.zeros((rows, 2 * Q), F32)
        for j in range(count):
            chosen = row == place_s[j:j + 1, :]
            prob = prob + jnp.where(chosen, pick_s[j:j + 1, :], 0.0)
            total = total + dot(one(chosen).astype(BF), blocks[FIRST[g] + j, 0:TOK, :])
        prob = jnp.sum(prob, axis=1, keepdims=True)
        prob_s[span(g), :] = prob
        rows_in[x, span(g), 0:Q] = total[:, 0:Q].astype(BF)
        rows_in[x, span(g), Q:2 * Q] = (total[:, Q:2 * Q] * prob).astype(BF)
        gathers[g, 0] = go(gather_copy(g, 0, x, 0, right))
        gathers[g, 1] = go(gather_copy(g, 1, x, 1, left))
        gathers[g, 2] = go(gather_copy(g, 2, x, 1, right))
        gathers[g, 3] = go(gather_copy(g, 3, x, 0, left))

    def forward(g):
        gathers[g, 0].wait_recv()
        gathers[g, 4] = go(gather_copy(g, 4, x_at(-1), 0, right))
        gathers[g, 1].wait_recv()
        gathers[g, 5] = go(gather_copy(g, 5, x_at(1), 1, left))

    def sum_copy(g, i, src, dst, device):
        return copy(src, dst, sum_s.at[6 * g + i], sum_r.at[6 * g + i], device)

    def part_at(g, q, part):
        return parts.at[q, span(g, part)]

    def compute(g):
        for i in (2, 3, 4, 5):
            gathers[g, i].wait_recv()
        if g == FIRST_COMPUTED:
            for c in loads[2:]:
                c.wait()
        gate = jnp.zeros((ROWS[g], Q), F32)
        up = jnp.zeros((ROWS[g], Q), F32)
        d_hidden = jnp.zeros((ROWS[g], Q), F32)
        for q in range(NX):
            latent = rows_in[q, span(g), 0:Q]
            gate = gate + dot(latent, wg_ref[q * Q:(q + 1) * Q, :])
            up = up + dot(latent, wu_ref[q * Q:(q + 1) * Q, :])
            d_hidden = d_hidden + dot_bt(rows_in[q, span(g), Q:2 * Q], wd_ref[:, q * Q:(q + 1) * Q])
        sigmoid = jax.nn.sigmoid(gate)
        activated = gate * sigmoid
        hidden = (activated * up).astype(BF)
        slope = sigmoid * (1.0 + gate * (1.0 - sigmoid))
        d_gate = (d_hidden * up * slope).astype(BF)
        d_up = (d_hidden * activated).astype(BF)
        hid_s[span(g), :] = hidden
        dgu_s[span(g), 0:Q] = d_gate
        dgu_s[span(g), Q:2 * Q] = d_up
        for q in range(NX):
            parts[q, span(g), 0:Q] = dot(hidden, wd_ref[:, q * Q:(q + 1) * Q]).astype(BF)
            back = dot_bt(d_gate, wg_ref[q * Q:(q + 1) * Q, :]) + dot_bt(d_up, wu_ref[q * Q:(q + 1) * Q, :])
            parts[q, span(g), Q:2 * Q] = back.astype(BF)
        sums[g, 0] = go(sum_copy(g, 0, part_at(g, x_at(2), 0), via.at[span(g, 0)], right))
        sums[g, 1] = go(sum_copy(g, 1, part_at(g, x_at(2), 1), via.at[span(g, 1)], left))
        sums[g, 2] = go(sum_copy(g, 2, part_at(g, x_at(1), 1), from_left.at[span(g, 1)], right))
        sums[g, 3] = go(sum_copy(g, 3, part_at(g, x_at(-1), 0), from_right.at[span(g, 0)], left))

    def pass_on(g):
        for part, q, dst, device in ((0, x_at(1), from_left, right), (1, x_at(-1), from_right, left)):
            sums[g, part].wait_recv()
            here = span(g, part)
            parts[q, here, :] = (parts[q, here, :].astype(F32) + via[here, :].astype(F32)).astype(BF)
            sums[g, 4 + part] = go(sum_copy(g, 4 + part, part_at(g, q, part), dst.at[here], device))

    returns = []

    def give_back(g):
        for i in (2, 3, 4, 5):
            sums[g, i].wait_recv()
        here = span(g)
        total = parts[x, here, :].astype(F32) + from_left[here, :].astype(F32) + from_right[here, :].astype(F32)
        scaled = (total[:, 0:Q] * prob_s[here, :]).astype(BF)
        plain = total[:, Q:2 * Q].astype(BF)
        size = BLOCKS[g] * SLOT
        packed = jnp.zeros((size, 128), F32)
        for c, values in enumerate((scaled[:, 0:128], scaled[:, 128:256], plain[:, 0:128], plain[:, 128:256])):
            packed = packed + dot(spread_s[c, 0:size, 0:ROWS[g]], values)
        back_out[FIRST[g] * SLOT:FIRST[g] * SLOT + size, :] = packed.astype(BF)
        target = pl.ds(pl.multiple_of(ep * SLOT, SLOT), SLOT)
        for offset in GROUPS[g]:
            for flip in (0, 1):
                i = INDEX[offset, flip]
                if i == own:
                    back_in[target, :] = back_out[i * SLOT:(i + 1) * SLOT, :]
                    continue
                returns.append(go(copy(back_out.at[pl.ds(i * SLOT, SLOT)], back_in.at[target],
                                       ret_s.at[i], ret_r.at[i], at_z(offset, flip))))

    trades = []

    def weight_gradients(_):
        for q in range(NX):
            both = dot_at(rows_in[q, :, 0:Q], dgu_s[...]).astype(BF)
            down = dot_at(hid_s[...], rows_in[q, :, Q:2 * Q]).astype(BF)
            for h in (0, 1):
                for c in range(4):
                    y_out[2 * q + h, c * 128:(c + 1) * 128, :] = both[h * 128:(h + 1) * 128, c * 128:(c + 1) * 128]
                y_out[2 * q + h, 512:768, :] = down[:, h * 128:(h + 1) * 128]
        for i in range(1, NY):
            to = lax.rem(y + i, NY)
            trades.append(go(copy(y_out.at[to], y_in.at[y], y_s.at[i], y_r.at[i], (ep, x, to))))

    steps = dict(r=ring, s=select, f=forward, c=compute, p=pass_on, g=give_back, w=weight_gradients)
    for word in ORDER.split():
        steps[word[0]](*[int(n) for n in word[1:].split(".")])

    y_in[y] = y_out[y]
    for trade in trades:
        trade.wait_recv()
    sum_y = jnp.zeros((768, 128), F32)
    for i in range(NY):
        sum_y = sum_y + y_in[i].astype(F32)
    gg_ref[0, :, 0:128] = sum_y[0:128]
    gg_ref[0, :, 128:256] = sum_y[128:256]
    gu_ref[0, :, 0:128] = sum_y[256:384]
    gu_ref[0, :, 128:256] = sum_y[384:512]
    gd_ref[0] = sum_y[512:768]
    for c in returns:
        c.wait_recv()
    for c, (ref, half) in enumerate(((comb_ref, 0), (comb_ref, 1), (glat_ref, 0), (glat_ref, 1))):
        ref[:, half * 128:(half + 1) * 128] = dot(tokens_s[c], back_in[...]).astype(BF)
    for c in sent:
        c.wait_send()


def local(latent, cotangent, expert_ids, route_probs, w_gate, w_up, w_down):
    vmem, anywhere = pl.BlockSpec(memory_space=pltpu.VMEM), pl.BlockSpec(memory_space=pl.ANY)
    dma = pltpu.SemaphoreType.DMA
    groups = len(GROUPS)
    shapes = (
        jax.ShapeDtypeStruct((TOK, Q), BF), jax.ShapeDtypeStruct((TOK, Q), BF),
        jax.ShapeDtypeStruct((1, 128, Q), F32), jax.ShapeDtypeStruct((1, 128, Q), F32),
        jax.ShapeDtypeStruct((1, Q, 128), F32))
    results = pl.pallas_call(
        body,
        out_shape=shapes,
        in_specs=[anywhere, anywhere, vmem, vmem, anywhere, anywhere, anywhere],
        out_specs=(vmem,) * 5,
        scratch_shapes=[
            pltpu.VMEM((32, TOK + META, 2 * Q), BF),
            pltpu.VMEM((NX, ALL, 2 * Q), BF),
            pltpu.VMEM((NX, ALL, 2 * Q), BF),
            pltpu.VMEM((ALL, 2 * Q), BF),
            pltpu.VMEM((ALL, 2 * Q), BF),
            pltpu.VMEM((ALL, 2 * Q), BF),
            pltpu.VMEM((32 * SLOT, 128), BF),
            pltpu.VMEM((32 * SLOT, 128), BF),
            pltpu.VMEM((NY, 768, 128), BF),
            pltpu.VMEM((NY, 768, 128), BF),
            pltpu.VMEM((ALL, Q), BF),
            pltpu.VMEM((ALL, 2 * Q), BF),
            pltpu.VMEM((ALL, 1), F32),
            pltpu.VMEM((16, TOK), F32),
            pltpu.VMEM((16, TOK), F32),
            pltpu.VMEM((16, TOK), F32),
            pltpu.VMEM((4, TOK, 32 * SLOT), BF),
            pltpu.VMEM((4, MOST * SLOT, max(ROWS)), BF),
            pltpu.VMEM((4 * Q, Q), BF), pltpu.VMEM((4 * Q, Q), BF), pltpu.VMEM((Q, 4 * Q), BF),
            dma((5,)), dma((32, len(CHUNKS) - 1)), dma((32, len(CHUNKS) - 1)),
            dma((6 * groups,)), dma((6 * groups,)), dma((6 * groups,)), dma((6 * groups,)),
            dma((32,)), dma((32,)), dma((NY,)), dma((NY,)),
        ],
        compiler_params=pltpu.CompilerParams(collective_id=0, has_side_effects=True, vmem_limit_bytes=56 * 2**20),
        cost_estimate=pl.CostEstimate(flops=4 * 10**9, bytes_accessed=8 * 2**20, transcendentals=10**6),
        name="moe",
    )(latent, cotangent, expert_ids.T, route_probs.T, w_gate[0], w_up[0], w_down[0])
    return pl.pallas_call(
        hand_over,
        out_shape=shapes,
        in_specs=[vmem] * 5,
        out_specs=(vmem,) * 5,
        name="results",
    )(*results)


def hand_over(*refs):
    for i in range(5):
        refs[5 + i][...] = refs[i][...]


def solution(mesh):
    return jax.shard_map(
        local,
        mesh=mesh,
        in_specs=(
            P(("ep", "dp"), None), P(("ep", "dp"), None), P(("ep", "dp"), None), P(("ep", "dp"), None),
            P("ep", None, "tp"), P("ep", None, "tp"), P("ep", "tp", None),
        ),
        out_specs=(
            P(("ep", "dp"), "tp"), P(("ep", "dp"), "tp"), P("ep", "dp", "tp"), P("ep", "dp", "tp"), P("ep", "tp", "dp"),
        ),
        check_vma=False,
    )
```
